256 devices in a mesh: ctx: 32 (over z, y), kvg: 8 (over x, core).
Axes of the slice: x: 4, y: 4, z: 8, core: 2. Of those that a mesh axis runs over, the one named last changes fastest.
Arguments:
- queries: bfloat16 [8192, 8192], P('ctx', 'kvg'), may hold values from -160 to 160
- keys: bfloat16 [8192, 1024], P(('ctx', 'kvg')), may hold values from -6 to 6
- values: bfloat16 [8192, 1024], P(('ctx', 'kvg')), may hold values from -6 to 6
- segment_ids: int32 [8192], replicated, may hold values from 0 to 11, never falling along the last dimension, each value on 1 to 2049 neighbouring positions
Outputs:
- attended: bfloat16 [8192, 8192], P('ctx', 'kvg')
The draws below stay inside these ranges and needn't reach their ends.
Inputs may be any that keep to these rules, and one draw needn't show every extreme that they name: `segment_ids`: prompt numbers never fall along the pack; each prompt has 1 to 2049 tokens, and one has exactly that many.
All inputs are finite; a program needn't handle non-finite values.
Results may differ from the reference program's by a relative error of at most 0.0019.
Values may be sent and summed in bfloat16 or wider, within the bound.
No kernel may reach another device: no remote copies, remote signals or barrier semaphores. Data moves between devices by JAX's collectives and lax.ppermute only.
A program may use at most 64 MiB of HBM per device.

```python
import math
import jax
import jax.numpy as jnp
import numpy as np
from jax import lax

QH = 64
KVH = 8
HEAD = 128
TOK_DEV = 256
DOCS = 12
REACH = 8
GROUP = 8
TOKENS = 8192


def shared_base(key):
    return jnp.clip(jax.random.normal(key, (TOKENS, KVH, HEAD), jnp.float32), -6.0, 6.0)


def draw_keys(key, part):
    base = shared_base(key)
    return base.reshape(TOKENS, KVH * HEAD).astype(jnp.bfloat16)


def draw_queries(key, part):
    base = shared_base(key)
    key = jax.random.fold_in(key, 12)
    noise = jnp.clip(jax.random.normal(key, (TOKENS, KVH, GROUP, HEAD), jnp.float32), -6.0, 6.0)
    result = 0.6 * base[:, :, None, :] + 0.8 * noise
    return result.reshape(TOKENS, QH * HEAD).astype(jnp.bfloat16)


def block_scale(stream_key, extent, split, smallest, largest):
    def one(dim, blocks):
        draws = jax.random.uniform(jax.random.fold_in(jax.random.fold_in(stream_key, 6), dim), (blocks,), jnp.float32, smallest / len(split), largest / len(split))
        return jnp.repeat(jnp.exp(draws), extent[dim] // blocks).reshape((-1,) + (1,) * (len(extent) - dim - 1))

    factor_of = one(*split[0])
    for cut in split[1:]:
        factor_of = factor_of * one(*cut)
    return factor_of


def profile(count, total, most, lean):
    portions = [(1 << 20) // math.isqrt(standing ** lean) + 1 for standing in range(2, count + 1)]
    spare, given = total - most - (count - 1), [1] * (count - 1)
    while spare > 0:
        candidates = [i for i in range(count - 1) if given[i] < most]
        mass, budget = sum([portions[i] for i in candidates]), spare
        for i in candidates:
            addition = min(most - given[i], max(1, budget * portions[i] // mass), spare)
            given[i] = given[i] + addition
            spare = spare - addition
    return np.array([most] + given)


def ragged_sizes(own_key, count, total, bound, lean):
    if count == 2:
        one = jax.random.randint(own_key, (), max(1, total - bound), min(bound, total - 1) + 1)
        return jnp.stack([one, total - one])
    lengths = jnp.asarray(profile(count, total, bound, lean), jnp.int32)
    couples = (count - 1) // 2
    source_of, taker = lengths[1:1 + 2 * couples:2], lengths[2:2 + 2 * couples:2]
    slack = jnp.minimum(source_of - 1, bound - taker)
    moved = jax.random.randint(jax.random.fold_in(own_key, 1), (couples,), 0, 1 << 20) % (slack + 1)
    lengths = lengths.at[1:1 + 2 * couples:2].set(source_of - moved).at[2:2 + 2 * couples:2].set(taker + moved)
    return lengths[jax.random.permutation(jax.random.fold_in(own_key, 2), count)]


def scatter_about(own_key, dims, width, reach, cuts=(), kind=jnp.bfloat16):
    gain = block_scale(own_key, dims, cuts, -0.22, 0.18) if cuts else 1.0
    drawn = jax.random.normal(own_key, dims, jnp.float32) * width * gain
    return jnp.minimum(jnp.maximum(drawn, -reach), reach).astype(kind)


def setup_inputs(seed: int = 0) -> dict:
    splits = jax.random.split(jax.random.key(seed), 5)
    return {
        "queries": draw_queries(jax.random.fold_in(splits[4], 71), 0),
        "keys": draw_keys(jax.random.fold_in(splits[4], 71), 0),
        "values": scatter_about(splits[2], (TOKENS, KVH * HEAD), 1.0, 6.0, ((0, 256),)),
        "segment_ids": jnp.searchsorted(jnp.cumsum(ragged_sizes(splits[3], DOCS, TOKENS, REACH * TOK_DEV + 1, 2)), jnp.arange(TOKENS), side="right").astype(jnp.int32),
    }


def block_part(q_part, k_part, v_part, allowed, scale_factor):
    scores = jnp.einsum("qgd,kd->gqk", q_part.astype(jnp.float32), k_part.astype(jnp.float32), precision=lax.Precision.HIGHEST) * scale_factor
    masked = jnp.where(allowed[None], scores, jnp.float32(-1e30))
    top = jnp.max(masked, axis=-1)
    expo = jnp.where(allowed[None], jnp.exp(masked - top[:, :, None]), jnp.float32(0.0))
    total = jnp.sum(expo, axis=-1)
    weights = expo.astype(jnp.bfloat16)
    partial_sum = jnp.einsum("gqk,kd->gqd", weights.astype(jnp.float32), v_part.astype(jnp.float32), precision=lax.Precision.HIGHEST)
    return partial_sum, top, total


def reference(queries, keys, values, segment_ids):
    total_rows = queries.shape[0]
    front = REACH * TOK_DEV
    scale_factor = 1.0 / (HEAD ** 0.5)
    segment_ids = segment_ids.astype(jnp.int32)
    key_pad = jnp.concatenate([jnp.zeros((front, keys.shape[1]), keys.dtype), keys], 0)
    value_pad = jnp.concatenate([jnp.zeros((front, values.shape[1]), values.dtype), values], 0)
    segment_pad = jnp.concatenate([jnp.full((front,), -1, jnp.int32), segment_ids], 0)

    def one_block(index):
        q_start = (index * TOK_DEV).astype(jnp.int32)
        query_rows = lax.dynamic_slice_in_dim(queries, q_start, TOK_DEV, 0)
        query_segs = lax.dynamic_slice_in_dim(segment_ids, q_start, TOK_DEV, 0)
        query_pos = q_start + jnp.arange(TOK_DEV, dtype=jnp.int32)
        pieces = [[] for head in range(KVH)]
        for back in range(REACH + 1):
            pad_start = (q_start + (REACH - back) * TOK_DEV).astype(jnp.int32)
            key_rows = lax.dynamic_slice_in_dim(key_pad, pad_start, TOK_DEV, 0)
            value_rows = lax.dynamic_slice_in_dim(value_pad, pad_start, TOK_DEV, 0)
            key_segs = lax.dynamic_slice_in_dim(segment_pad, pad_start, TOK_DEV, 0)
            key_pos = q_start - back * TOK_DEV + jnp.arange(TOK_DEV, dtype=jnp.int32)
            allowed = (query_segs[:, None] == key_segs[None, :]) & (key_pos[None, :] <= query_pos[:, None])
            for head in range(KVH):
                q_part = query_rows[:, head * GROUP * HEAD:(head + 1) * GROUP * HEAD].reshape(TOK_DEV, GROUP, HEAD)
                k_part = key_rows[:, head * HEAD:(head + 1) * HEAD]
                v_part = value_rows[:, head * HEAD:(head + 1) * HEAD]
                pieces[head].append(block_part(q_part, k_part, v_part, allowed, scale_factor))
        outputs = []
        for head in range(KVH):
            best = pieces[head][0][1]
            for member in pieces[head][1:]:
                best = jnp.maximum(best, member[1])
            numer = jnp.zeros((GROUP, TOK_DEV, HEAD), jnp.float32)
            denom = jnp.zeros((GROUP, TOK_DEV), jnp.float32)
            for partial_sum, top, total in pieces[head]:
                factor = jnp.where(total > 0, jnp.exp(top - best), jnp.float32(0.0))
                numer = numer + factor[:, :, None] * partial_sum
                denom = denom + factor * total
            mixed = numer / denom[:, :, None]
            outputs.append(jnp.transpose(mixed, (1, 0, 2)).astype(jnp.bfloat16).reshape(TOK_DEV, GROUP * HEAD))
        return jnp.concatenate(outputs, 1)

    blocks = lax.map(one_block, jnp.arange(total_rows // TOK_DEV, dtype=jnp.int32))
    return blocks.reshape(total_rows, QH * HEAD)
```

```python
import functools

import jax
import jax.numpy as jnp
import numpy as np
from jax import lax
from jax.experimental import pallas as pl
from jax.experimental.pallas import tpu as pltpu
from jax.sharding import PartitionSpec as P

HEAD = 128
EXP2_SCALE = float(np.log2(np.e) / np.sqrt(HEAD))
MASKED = -1e30
NT = (((1,), (1,)), ((), ()))
WIDE = 4
VMEM = pl.BlockSpec(memory_space=pltpu.VMEM)
SMEM = pl.BlockSpec(memory_space=pltpu.SMEM)


def pack_kernel(groups, k_ref, v_ref, o_ref):
    for g in range(groups):
        o_ref[g, 0] = k_ref[:, g * HEAD : (g + 1) * HEAD]
        o_ref[g, 1] = v_ref[:, g * HEAD : (g + 1) * HEAD]


def pack(keys, values):
    rows, columns = keys.shape
    groups = columns // HEAD
    return pl.pallas_call(
        functools.partial(pack_kernel, groups),
        in_specs=[VMEM, VMEM],
        out_specs=VMEM,
        out_shape=jax.ShapeDtypeStruct((groups, 2, rows, HEAD), keys.dtype),
    )(keys, values)


def outgoing_kernel(shifts, position_ref, own_ref, near_ref, far_ref, *out_refs):
    y = lax.rem(position_ref[0], WIDE)
    for shift, out in zip(shifts, out_refs):
        out[0] = near_ref[...]
        target = lax.rem(y + shift, WIDE)

        @pl.when(y < target)
        def _():
            out[1] = own_ref[...]

        @pl.when(y > target)
        def _():
            out[1] = far_ref[...]


def outgoing(position, own, near, far, shifts):
    shape = jax.ShapeDtypeStruct((2, *own.shape), own.dtype)
    return pl.pallas_call(
        functools.partial(outgoing_kernel, shifts),
        in_specs=[SMEM, VMEM, VMEM, VMEM],
        out_specs=[VMEM] * len(shifts),
        out_shape=[shape] * len(shifts),
    )(position, own, near, far)


def attend_kernel(plan, per_item, own, has_state, final, *refs):
    refs = list(refs)
    position_ref, q_ref, seg_ref = refs[:3]
    buffers = 1 + max(b for b, _, _ in plan)
    kv_refs = refs[3 : 3 + buffers]
    refs = refs[3 + buffers :]
    if has_state:
        acc_in, stat_in = refs[:2]
        refs = refs[2:]
    if final:
        out_ref = refs[0]
        refs = refs[1:]
    else:
        acc_out, stat_out = refs[:2]
        refs = refs[2:]
    k_s, vt_s, bias_s, s_s, p_s, t_s, acc_s = refs

    rows = q_ref.shape[0]
    heads = q_ref.shape[1] // HEAD
    count = len(plan)
    c = position_ref[0]
    q_seg = seg_ref[pl.ds(c, 1), :]
    first_seg = jnp.min(q_seg)
    start = jnp.sum((seg_ref[...] < first_seg).astype(jnp.int32))
    query_bias = jnp.where(q_seg == first_seg, 0.0, MASKED).astype(jnp.float32)
    for i, (b, slot, block_of) in enumerate(plan):
        src = kv_refs[b] if slot is None else kv_refs[b].at[slot]
        k_s[i * rows : (i + 1) * rows] = src[:, 0].reshape(rows, HEAD)
        vt_s[:, i * rows : (i + 1) * rows] = src[:, 1].reshape(rows, HEAD).T
        if own:
            key_seg = jnp.broadcast_to(q_seg.astype(jnp.float32), (rows, rows)).T
            k_pos = lax.broadcasted_iota(jnp.int32, (rows, rows), 0)
            q_pos = lax.broadcasted_iota(jnp.int32, (rows, rows), 1)
            allowed = (key_seg == q_seg.astype(jnp.float32)) & (k_pos <= q_pos)
            bias_s[...] = jnp.where(allowed, 0.0, MASKED).astype(jnp.float32)
        else:
            k_pos = block_of(c) * rows + lax.broadcasted_iota(jnp.int32, (rows, HEAD), 0)
            bias_s[i * rows : (i + 1) * rows] = jnp.where(k_pos >= start, 0.0, MASKED).astype(
                jnp.float32
            )

    splits = count // per_item
    items = [(h, g) for h in range(heads) for g in range(splits)]

    def score(t):
        h, g = items[t]
        s_s[t % 2] = lax.dot_general(
            k_s[g * per_item * rows : (g + 1) * per_item * rows],
            q_ref[:, h * HEAD : (h + 1) * HEAD],
            NT,
            preferred_element_type=jnp.float32,
        )

    def soften(t):
        _, g = items[t]
        for i in range(per_item):
            x = s_s[t % 2, i * rows : (i + 1) * rows]
            at = (g * per_item + i) * rows
            bias = bias_s[at : at + rows]
            x = x + (bias if own else jnp.concatenate([bias] * (rows // HEAD), 1))
            top = jnp.max(x, 0, keepdims=True)
            expo = jnp.exp2((x - top) * EXP2_SCALE)
            t_s[t % 2, i : i + 1] = top if own else top + query_bias
            t_s[t % 2, 8 + i : 9 + i] = jnp.sum(expo, 0, keepdims=True)
            p_s[t % 2, i * rows : (i + 1) * rows] = expo.astype(jnp.bfloat16)

    def mix(t):
        h, g = items[t]
        tops = [t_s[t % 2, i : i + 1] for i in range(per_item)]
        totals = [t_s[t % 2, 8 + i : 9 + i] for i in range(per_item)]
        best = functools.reduce(jnp.maximum, tops)
        acc = total = None
        if g > 0:
            old = t_s[2 + h % 2, 0:1]
            best = jnp.maximum(best, old)
            f = jnp.exp2((old - best) * EXP2_SCALE)
            acc, total = acc_s[h % 2] * f, t_s[2 + h % 2, 8:9] * f
        elif has_state:
            old = stat_in[h, 0:1]
            best = jnp.maximum(best, old)
            f = jnp.exp2((old - best) * EXP2_SCALE)
            acc, total = acc_in[h] * f, stat_in[h, 1:2] * f
        for i in range(per_item):
            at = (g * per_item + i) * rows
            part = jnp.dot(
                vt_s[:, at : at + rows],
                p_s[t % 2, i * rows : (i + 1) * rows],
                preferred_element_type=jnp.float32,
            )
            f = jnp.exp2((tops[i] - best) * EXP2_SCALE)
            acc = part * f if acc is None else acc + part * f
            total = totals[i] * f if total is None else total + totals[i] * f
        if g < splits - 1:
            acc_s[h % 2] = acc
            t_s[2 + h % 2, 0:1] = best
            t_s[2 + h % 2, 8:9] = total
        elif final:
            out_ref[:, h * HEAD : (h + 1) * HEAD] = (acc / total).T.astype(jnp.bfloat16)
        else:
            acc_out[h] = acc
            stat_out[h, 0:1] = best
            stat_out[h, 1:2] = total

    for t in range(len(items) + 2):
        if t >= 2:
            mix(t - 2)
        if 1 <= t <= len(items):
            soften(t - 1)
        if t < len(items):
            score(t)


def attend(position, queries, segments, buffers, plan, per_item, own=False, state=(), final=False):
    rows, columns = queries.shape
    heads = columns // HEAD
    count = len(plan)
    if final:
        out_shape = jax.ShapeDtypeStruct(queries.shape, queries.dtype)
        out_specs = VMEM
    else:
        out_shape = [
            jax.ShapeDtypeStruct((heads, HEAD, rows), jnp.float32),
            jax.ShapeDtypeStruct((heads, 8, rows), jnp.float32),
        ]
        out_specs = [VMEM, VMEM]
    return pl.pallas_call(
        functools.partial(attend_kernel, plan, per_item, own, bool(state), final),
        in_specs=[SMEM] + [VMEM] * (2 + len(buffers) + len(state)),
        out_specs=out_specs,
        out_shape=out_shape,
        scratch_shapes=[
            pltpu.VMEM((count * rows, HEAD), jnp.bfloat16),
            pltpu.VMEM((HEAD, count * rows), jnp.bfloat16),
            pltpu.VMEM((count * rows, rows if own else HEAD), jnp.float32),
            pltpu.VMEM((2, per_item * rows, rows), jnp.float32),
            pltpu.VMEM((2, per_item * rows, rows), jnp.bfloat16),
            pltpu.VMEM((4, 16, rows), jnp.float32),
            pltpu.VMEM((2, HEAD, rows), jnp.float32),
        ],
        compiler_params=pltpu.CompilerParams(vmem_limit_bytes=24 << 20),
        cost_estimate=pl.CostEstimate(
            flops=4 * heads * rows * rows * HEAD * count,
            bytes_accessed=4 * rows * columns,
            transcendentals=heads * rows * rows * count,
        ),
    )(position, queries, segments, *buffers, *state)


def own_block(c):
    return c


def back_block(distance, c):
    return c - distance


def near_row(shift, c):
    y = lax.rem(c, WIDE)
    source = lax.rem(y - shift + WIDE, WIDE)
    return c - y + source - WIDE


def edge_row(shift, c):
    y = lax.rem(c, WIDE)
    source = lax.rem(y - shift + WIDE, WIDE)
    return c - y + source - jnp.where(source < y, 0, 2 * WIDE)


def on_device(queries, keys, values, segment_ids):
    rows = queries.shape[0]
    blocks = lax.axis_size("ctx")
    position = lax.axis_index("ctx").astype(jnp.int32).reshape(1)
    segments = segment_ids.reshape(blocks, rows)
    own = lax.all_to_all(pack(keys, values), "kvg", split_axis=0, concat_axis=0, tiled=True)

    def back(block, distance):
        return lax.ppermute(block, "ctx", [(i, (i + distance) % blocks) for i in range(blocks)])

    def around(block, shift):
        return lax.ppermute(
            block, "ctx", [(i, i - i % WIDE + (i + shift) % WIDE) for i in range(blocks)]
        )

    near = back(own, WIDE)
    far = back(own, 2 * WIDE)
    state = attend(position, queries, segments, [own], [(0, None, own_block)], 1, own=True)
    shifts = (1, 3, 2)
    arrived = [
        around(block, shift)
        for block, shift in zip(outgoing(position, own, near, far, shifts), shifts)
    ]
    plan = [
        (0, None, functools.partial(back_block, WIDE)),
        (1, None, functools.partial(back_block, 2 * WIDE)),
    ]
    state = attend(position, queries, segments, [near, far], plan, 2, state=state)
    plan = []
    for i, shift in enumerate(shifts):
        plan.append((i, 0, functools.partial(near_row, shift)))
        plan.append((i, 1, functools.partial(edge_row, shift)))
    return attend(position, queries, segments, arrived, plan, 3, state=state, final=True)


def solution(mesh):
    return jax.shard_map(
        on_device,
        mesh=mesh,
        in_specs=(P("ctx", "kvg"), P(("ctx", "kvg"), None), P(("ctx", "kvg"), None), P()),
        out_specs=P("ctx", "kvg"),
        check_vma=False,
    )
```

```python
import functools

import jax
import jax.numpy as jnp
import numpy as np
from jax import lax
from jax.experimental import pallas as pl
from jax.experimental.pallas import tpu as pltpu
from jax.sharding import PartitionSpec as P

HEAD = 128
EXP2_SCALE = float(np.log2(np.e) / np.sqrt(HEAD))
MASKED = -1e30
NT = (((1,), (1,)), ((), ()))
WIDE = 4
VMEM = pl.BlockSpec(memory_space=pltpu.VMEM)
SMEM = pl.BlockSpec(memory_space=pltpu.SMEM)


def pack_kernel(groups, k_ref, v_ref, o_ref):
    for g in range(groups):
        o_ref[g, 0] = k_ref[:, g * HEAD : (g + 1) * HEAD]
        o_ref[g, 1] = v_ref[:, g * HEAD : (g + 1) * HEAD]


def pack(keys, values):
    rows, columns = keys.shape
    groups = columns // HEAD
    return pl.pallas_call(
        functools.partial(pack_kernel, groups),
        in_specs=[VMEM, VMEM],
        out_specs=VMEM,
        out_shape=jax.ShapeDtypeStruct((groups, 2, rows, HEAD), keys.dtype),
    )(keys, values)


def attend_kernel(plan, per_item, own, has_state, final, *refs):
    refs = list(refs)
    position_ref, q_ref, seg_ref = refs[:3]
    buffers = 1 + max(b for b, _, _ in plan)
    kv_refs = refs[3 : 3 + buffers]
    refs = refs[3 + buffers :]
    if has_state:
        acc_in, stat_in = refs[:2]
        refs = refs[2:]
    if final:
        out_ref = refs[0]
        refs = refs[1:]
    else:
        acc_out, stat_out = refs[:2]
        refs = refs[2:]
    k_s, vt_s, bias_s, s_s, p_s, t_s, acc_s = refs

    rows = q_ref.shape[0]
    heads = q_ref.shape[1] // HEAD
    count = len(plan)
    c = position_ref[0]
    q_seg = seg_ref[pl.ds(c, 1), :]
    first_seg = jnp.min(q_seg)
    start = jnp.sum((seg_ref[...] < first_seg).astype(jnp.int32))
    query_bias = jnp.where(q_seg == first_seg, 0.0, MASKED).astype(jnp.float32)
    for i, (b, slot, block_of) in enumerate(plan):
        src = kv_refs[b] if slot is None else kv_refs[b].at[slot]
        k_s[i * rows : (i + 1) * rows] = src[:, 0].reshape(rows, HEAD)
        vt_s[:, i * rows : (i + 1) * rows] = src[:, 1].reshape(rows, HEAD).T
        if own:
            key_seg = jnp.broadcast_to(q_seg.astype(jnp.float32), (rows, rows)).T
            k_pos = lax.broadcasted_iota(jnp.int32, (rows, rows), 0)
            q_pos = lax.broadcasted_iota(jnp.int32, (rows, rows), 1)
            allowed = (key_seg == q_seg.astype(jnp.float32)) & (k_pos <= q_pos)
            bias_s[...] = jnp.where(allowed, 0.0, MASKED).astype(jnp.float32)
        else:
            k_pos = block_of(c) * rows + lax.broadcasted_iota(jnp.int32, (rows, HEAD), 0)
            bias_s[i * rows : (i + 1) * rows] = jnp.where(k_pos >= start, 0.0, MASKED).astype(
                jnp.float32
            )

    splits = count // per_item
    items = [(h, g) for h in range(heads) for g in range(splits)]

    def score(t):
        h, g = items[t]
        s_s[t % 2] = lax.dot_general(
            k_s[g * per_item * rows : (g + 1) * per_item * rows],
            q_ref[:, h * HEAD : (h + 1) * HEAD],
            NT,
            preferred_element_type=jnp.float32,
        )

    def soften(t):
        _, g = items[t]
        for i in range(per_item):
            x = s_s[t % 2, i * rows : (i + 1) * rows]
            at = (g * per_item + i) * rows
            bias = bias_s[at : at + rows]
            x = x + (bias if own else jnp.concatenate([bias] * (rows // HEAD), 1))
            top = jnp.max(x, 0, keepdims=True)
            expo = jnp.exp2((x - top) * EXP2_SCALE)
            t_s[t % 2, i : i + 1] = top if own else top + query_bias
            t_s[t % 2, 8 + i : 9 + i] = jnp.sum(expo, 0, keepdims=True)
            p_s[t % 2, i * rows : (i + 1) * rows] = expo.astype(jnp.bfloat16)

    def mix(t):
        h, g = items[t]
        tops = [t_s[t % 2, i : i + 1] for i in range(per_item)]
        totals = [t_s[t % 2, 8 + i : 9 + i] for i in range(per_item)]
        best = functools.reduce(jnp.maximum, tops)
        acc = total = None
        if g > 0:
            old = t_s[2 + h % 2, 0:1]
            best = jnp.maximum(best, old)
            f = jnp.exp2((old - best) * EXP2_SCALE)
            acc, total = acc_s[h % 2] * f, t_s[2 + h % 2, 8:9] * f
        elif has_state:
            old = stat_in[h, 0:1]
            best = jnp.maximum(best, old)
            f = jnp.exp2((old - best) * EXP2_SCALE)
            acc, total = acc_in[h] * f, stat_in[h, 1:2] * f
        for i in range(per_item):
            at = (g * per_item + i) * rows
            part = jnp.dot(
                vt_s[:, at : at + rows],
                p_s[t % 2, i * rows : (i + 1) * rows],
                preferred_element_type=jnp.float32,
            )
            f = jnp.exp2((tops[i] - best) * EXP2_SCALE)
            acc = part * f if acc is None else acc + part * f
            total = totals[i] * f if total is None else total + totals[i] * f
        if g < splits - 1:
            acc_s[h % 2] = acc
            t_s[2 + h % 2, 0:1] = best
            t_s[2 + h % 2, 8:9] = total
        elif final:
            out_ref[:, h * HEAD : (h + 1) * HEAD] = (acc / total).T.astype(jnp.bfloat16)
        else:
            acc_out[h] = acc
            stat_out[h, 0:1] = best
            stat_out[h, 1:2] = total

    for t in range(len(items) + 2):
        if t >= 2:
            mix(t - 2)
        if 1 <= t <= len(items):
            soften(t - 1)
        if t < len(items):
            score(t)


def attend(position, queries, segments, buffers, plan, per_item, own=False, state=(), final=False):
    rows, columns = queries.shape
    heads = columns // HEAD
    count = len(plan)
    if final:
        out_shape = jax.ShapeDtypeStruct(queries.shape, queries.dtype)
        out_specs = VMEM
    else:
        out_shape = [
            jax.ShapeDtypeStruct((heads, HEAD, rows), jnp.float32),
            jax.ShapeDtypeStruct((heads, 8, rows), jnp.float32),
        ]
        out_specs = [VMEM, VMEM]
    return pl.pallas_call(
        functools.partial(attend_kernel, plan, per_item, own, bool(state), final),
        in_specs=[SMEM] + [VMEM] * (2 + len(buffers) + len(state)),
        out_specs=out_specs,
        out_shape=out_shape,
        scratch_shapes=[
            pltpu.VMEM((count * rows, HEAD), jnp.bfloat16),
            pltpu.VMEM((HEAD, count * rows), jnp.bfloat16),
            pltpu.VMEM((count * rows, rows if own else HEAD), jnp.float32),
            pltpu.VMEM((2, per_item * rows, rows), jnp.float32),
            pltpu.VMEM((2, per_item * rows, rows), jnp.bfloat16),
            pltpu.VMEM((4, 16, rows), jnp.float32),
            pltpu.VMEM((2, HEAD, rows), jnp.float32),
        ],
        compiler_params=pltpu.CompilerParams(vmem_limit_bytes=24 << 20),
        cost_estimate=pl.CostEstimate(
            flops=4 * heads * rows * rows * HEAD * count,
            bytes_accessed=4 * rows * columns,
            transcendentals=heads * rows * rows * count,
        ),
    )(position, queries, segments, *buffers, *state)


def own_block(c):
    return c


def back_block(distance, c):
    return c - distance


def near_row(shift, c):
    y = lax.rem(c, WIDE)
    source = lax.rem(y - shift + WIDE, WIDE)
    return c - y + source - WIDE


def edge_row(shift, c):
    y = lax.rem(c, WIDE)
    source = lax.rem(y - shift + WIDE, WIDE)
    return c - y + source - jnp.where(source < y, 0, 2 * WIDE)


def on_device(queries, keys, values, segment_ids):
    rows = queries.shape[0]
    blocks = lax.axis_size("ctx")
    position = lax.axis_index("ctx").astype(jnp.int32).reshape(1)
    segments = segment_ids.reshape(blocks, rows)
    own = lax.all_to_all(pack(keys, values), "kvg", split_axis=0, concat_axis=0, tiled=True)

    def back(block, distance):
        return lax.ppermute(block, "ctx", [(i, (i + distance) % blocks) for i in range(blocks)])

    def around(block, shift):
        return lax.ppermute(
            block, "ctx", [(i, i - i % WIDE + (i + shift) % WIDE) for i in range(blocks)]
        )

    y = lax.rem(position[0], WIDE)
    near = back(own, WIDE)
    state = attend(position, queries, segments, [own], [(0, None, own_block)], 1, own=True)
    shifts = (1, 3, 2)
    near_arrived = [around(near, shift) for shift in shifts]
    far = back(near, WIDE)
    edge_arrived = [
        around(jnp.where(y < lax.rem(y + shift, WIDE), own, far), shift) for shift in shifts
    ]
    plan = [
        (0, None, functools.partial(back_block, WIDE)),
        (1, None, functools.partial(back_block, 2 * WIDE)),
    ]
    state = attend(position, queries, segments, [near, far], plan, 2, state=state)
    plan = [(i, None, functools.partial(near_row, shift)) for i, shift in enumerate(shifts)]
    state = attend(position, queries, segments, near_arrived, plan, 3, state=state)
    plan = [(i, None, functools.partial(edge_row, shift)) for i, shift in enumerate(shifts)]
    return attend(position, queries, segments, edge_arrived, plan, 3, state=state, final=True)


def solution(mesh):
    return jax.shard_map(
        on_device,
        mesh=mesh,
        in_specs=(P("ctx", "kvg"), P(("ctx", "kvg"), None), P(("ctx", "kvg"), None), P()),
        out_specs=P("ctx", "kvg"),
        check_vma=False,
    )
```

```python
import functools

import jax
import jax.numpy as jnp
import numpy as np
from jax import lax
from jax.experimental import pallas as pl
from jax.experimental.pallas import tpu as pltpu
from jax.sharding import PartitionSpec as P

HEAD = 128
EXP2_SCALE = float(np.log2(np.e) / np.sqrt(HEAD))
MASKED = -1e30
NT = (((1,), (1,)), ((), ()))
WIDE = 4
VMEM = pl.BlockSpec(memory_space=pltpu.VMEM)
SMEM = pl.BlockSpec(memory_space=pltpu.SMEM)


def pack_kernel(groups, k_ref, v_ref, o_ref):
    for g in range(groups):
        o_ref[g, 0] = k_ref[:, g * HEAD : (g + 1) * HEAD]
        o_ref[g, 1] = v_ref[:, g * HEAD : (g + 1) * HEAD]


def pack(keys, values):
    rows, columns = keys.shape
    groups = columns // HEAD
    return pl.pallas_call(
        functools.partial(pack_kernel, groups),
        in_specs=[VMEM, VMEM],
        out_specs=VMEM,
        out_shape=jax.ShapeDtypeStruct((groups, 2, rows, HEAD), keys.dtype),
    )(keys, values)


def attend_kernel(plan, per_item, own, has_state, final, *refs):
    refs = list(refs)
    position_ref, q_ref, seg_ref = refs[:3]
    buffers = 1 + max(b for b, _, _ in plan)
    kv_refs = refs[3 : 3 + buffers]
    refs = refs[3 + buffers :]
    if has_state:
        acc_in, stat_in = refs[:2]
        refs = refs[2:]
    if final:
        out_ref = refs[0]
        refs = refs[1:]
    else:
        acc_out, stat_out = refs[:2]
        refs = refs[2:]
    k_s, vt_s, bias_s, one_s, s_s, p_s, t_s, acc_s, *rest = refs

    rows = q_ref.shape[0]
    heads = q_ref.shape[1] // HEAD
    count = len(plan)
    c = position_ref[0]
    parts = rows // HEAD
    q_seg = jnp.concatenate([seg_ref[pl.ds(parts * c + i, 1), :] for i in range(parts)], 1)
    first_seg = jnp.min(q_seg)
    start = jnp.sum((seg_ref[...] < first_seg).astype(jnp.int32))
    query_bias = jnp.where(q_seg == first_seg, 0.0, MASKED).astype(jnp.float32)
    for i, (b, slot, block_of) in enumerate(plan):
        src = kv_refs[b] if slot is None else kv_refs[b].at[slot]
        k_s[i * rows : (i + 1) * rows, :HEAD] = src[:, 0].reshape(rows, HEAD)
        vt_s[:, i * rows : (i + 1) * rows] = src[:, 1].reshape(rows, HEAD).T
        if own:
            key_seg = jnp.broadcast_to(q_seg.astype(jnp.float32), (rows, rows)).T
            k_pos = lax.broadcasted_iota(jnp.int32, (rows, rows), 0)
            q_pos = lax.broadcasted_iota(jnp.int32, (rows, rows), 1)
            allowed = (key_seg == q_seg.astype(jnp.float32)) & (k_pos <= q_pos)
            bias_s[...] = jnp.where(allowed, 0.0, MASKED).astype(jnp.float32)
        else:
            lane = lax.broadcasted_iota(jnp.int32, (rows, HEAD), 1)
            k_pos = block_of(c) * rows + lax.broadcasted_iota(jnp.int32, (rows, HEAD), 0)
            masked = (k_pos < start) & (lane == 0)
            k_s[i * rows : (i + 1) * rows, HEAD:] = jnp.where(masked, MASKED, 0.0).astype(
                jnp.bfloat16
            )
            one_s[...] = jnp.where(lane == 0, 1.0, 0.0).astype(jnp.bfloat16)

    splits = count // per_item
    items = [(h, g) for h in range(heads) for g in range(splits)]

    def score(t):
        h, g = items[t]
        q = q_ref[:, h * HEAD : (h + 1) * HEAD]
        if not own:
            q = jnp.concatenate([q, one_s[...]], 1)
        s_s[t % 2] = lax.dot_general(
            k_s[g * per_item * rows : (g + 1) * per_item * rows],
            q,
            NT,
            preferred_element_type=jnp.float32,
        )

    def soften(t):
        _, g = items[t]
        for i in range(per_item):
            x = s_s[t % 2, i * rows : (i + 1) * rows]
            if own:
                x = x + bias_s[...]
            top = jnp.max(x, 0, keepdims=True)
            expo = jnp.exp2((x - top) * EXP2_SCALE)
            t_s[t % 2, i : i + 1] = top if own else top + query_bias
            t_s[t % 2, 8 + i : 9 + i] = jnp.sum(expo, 0, keepdims=True)
            p_s[t % 2, i * rows : (i + 1) * rows] = expo.astype(jnp.bfloat16)

    def mix(t):
        h, g = items[t]
        tops = [t_s[t % 2, i : i + 1] for i in range(per_item)]
        totals = [t_s[t % 2, 8 + i : 9 + i] for i in range(per_item)]
        best = functools.reduce(jnp.maximum, tops)
        acc = total = None
        if g > 0:
            old = t_s[2 + h % 2, 0:1]
            best = jnp.maximum(best, old)
            f = jnp.exp2((old - best) * EXP2_SCALE)
            acc, total = acc_s[h % 2] * f, t_s[2 + h % 2, 8:9] * f
        elif has_state:
            old = stat_in[h, 0:1]
            best = jnp.maximum(best, old)
            f = jnp.exp2((old - best) * EXP2_SCALE)
            acc, total = acc_in[h] * f, stat_in[h, 1:2] * f
        for i in range(per_item):
            at = (g * per_item + i) * rows
            part = jnp.dot(
                vt_s[:, at : at + rows],
                p_s[t % 2, i * rows : (i + 1) * rows],
                preferred_element_type=jnp.float32,
            )
            f = jnp.exp2((tops[i] - best) * EXP2_SCALE)
            acc = part * f if acc is None else acc + part * f
            total = totals[i] * f if total is None else total + totals[i] * f
        if g < splits - 1:
            acc_s[h % 2] = acc
            t_s[2 + h % 2, 0:1] = best
            t_s[2 + h % 2, 8:9] = total
        elif final:
            out_s, sems = rest
            out_s[h] = (acc / total).astype(jnp.bfloat16).T
            copies.append(
                pltpu.make_async_copy(
                    out_s.at[h], out_ref.at[:, h * HEAD : (h + 1) * HEAD], sems.at[h]
                )
            )
            copies[-1].start()
        else:
            acc_out[h] = acc
            stat_out[h, 0:1] = best
            stat_out[h, 1:2] = total

    copies = []
    for t in range(len(items) + 2):
        if t < len(items):
            score(t)
        if 1 <= t <= len(items):
            soften(t - 1)
        if t >= 2:
            mix(t - 2)
    for copy in copies:
        copy.wait()


def attend(position, queries, segments, buffers, plan, per_item, own=False, state=(), final=False):
    rows, columns = queries.shape
    heads = columns // HEAD
    count = len(plan)
    if final:
        out_shape = jax.ShapeDtypeStruct(queries.shape, queries.dtype)
        out_specs = pl.BlockSpec(memory_space=pl.ANY)
    else:
        out_shape = [
            jax.ShapeDtypeStruct((heads, HEAD, rows), jnp.float32),
            jax.ShapeDtypeStruct((heads, 8, rows), jnp.float32),
        ]
        out_specs = [VMEM, VMEM]
    return pl.pallas_call(
        functools.partial(attend_kernel, plan, per_item, own, bool(state), final),
        in_specs=[SMEM] + [VMEM] * (2 + len(buffers) + len(state)),
        out_specs=out_specs,
        out_shape=out_shape,
        scratch_shapes=[
            pltpu.VMEM((count * rows, HEAD if own else 2 * HEAD), jnp.bfloat16),
            pltpu.VMEM((HEAD, count * rows), jnp.bfloat16),
            pltpu.VMEM((rows, rows if own else HEAD), jnp.float32),
            pltpu.VMEM((rows, HEAD), jnp.bfloat16),
            pltpu.VMEM((2, per_item * rows, rows), jnp.float32),
            pltpu.VMEM((2, per_item * rows, rows), jnp.bfloat16),
            pltpu.VMEM((4, 16, rows), jnp.float32),
            pltpu.VMEM((2, HEAD, rows), jnp.float32),
        ]
        + (
            [pltpu.VMEM((heads, rows, HEAD), queries.dtype), pltpu.SemaphoreType.DMA((heads,))]
            if final
            else []
        ),
        compiler_params=pltpu.CompilerParams(vmem_limit_bytes=24 << 20),
        cost_estimate=pl.CostEstimate(
            flops=4 * heads * rows * rows * HEAD * count,
            bytes_accessed=4 * rows * columns,
            transcendentals=heads * rows * rows * count,
        ),
    )(position, queries, segments, *buffers, *state)


def own_block(c):
    return c


def back_block(distance, c):
    return c - distance


def near_row(shift, c):
    y = lax.rem(c, WIDE)
    source = lax.rem(y - shift + WIDE, WIDE)
    return c - y + source - WIDE


def edge_row(shift, c):
    y = lax.rem(c, WIDE)
    source = lax.rem(y - shift + WIDE, WIDE)
    return c - y + source - jnp.where(source < y, 0, 2 * WIDE)


def on_device(queries, keys, values, segment_ids):
    rows = queries.shape[0]
    blocks = lax.axis_size("ctx")
    position = lax.axis_index("ctx").astype(jnp.int32).reshape(1)
    segments = segment_ids.reshape(-1, HEAD)
    own = lax.all_to_all(pack(keys, values), "kvg", split_axis=0, concat_axis=0, tiled=True)

    def back(block, distance):
        return lax.ppermute(block, "ctx", [(i, (i + distance) % blocks) for i in range(blocks)])

    def around(block, shift):
        return lax.ppermute(
            block, "ctx", [(i, i - i % WIDE + (i + shift) % WIDE) for i in range(blocks)]
        )

    y = lax.rem(position[0], WIDE)
    near = back(own, WIDE)
    state = attend(position, queries, segments, [own], [(0, None, own_block)], 1, own=True)
    near, state = lax.optimization_barrier((near, state))
    shifts = (1, 3, 2)
    near_arrived = [around(near, shift) for shift in shifts]
    far = back(near, WIDE)
    edge_arrived = [
        around(jnp.where(y < lax.rem(y + shift, WIDE), own, far), shift) for shift in shifts
    ]
    plan = [
        (0, None, functools.partial(back_block, WIDE)),
        (1, None, functools.partial(back_block, 2 * WIDE)),
    ]
    plan += [(2 + i, None, functools.partial(near_row, shift)) for i, shift in enumerate(shifts)]
    state = attend(position, queries, segments, [near, far, *near_arrived], plan, 5, state=state)
    plan = [(i, None, functools.partial(edge_row, shift)) for i, shift in enumerate(shifts)]
    return attend(position, queries, segments, edge_arrived, plan, 3, state=state, final=True)


def solution(mesh):
    return jax.shard_map(
        on_device,
        mesh=mesh,
        in_specs=(P("ctx", "kvg"), P(("ctx", "kvg"), None), P(("ctx", "kvg"), None), P()),
        out_specs=P("ctx", "kvg"),
        check_vma=False,
    )
```

```python
import functools

import jax
import jax.numpy as jnp
import numpy as np
from jax import lax
from jax.experimental import pallas as pl
from jax.experimental.pallas import tpu as pltpu
from jax.sharding import PartitionSpec as P

HEAD = 128
EXP2_SCALE = float(np.log2(np.e) / np.sqrt(HEAD))
MASKED = -1e30
NT = (((1,), (1,)), ((), ()))
WIDE = 4
VMEM = pl.BlockSpec(memory_space=pltpu.VMEM)
SMEM = pl.BlockSpec(memory_space=pltpu.SMEM)


def pack_kernel(groups, k_ref, v_ref, o_ref):
    for g in range(groups):
        o_ref[g, 0] = k_ref[:, g * HEAD : (g + 1) * HEAD]
        o_ref[g, 1] = v_ref[:, g * HEAD : (g + 1) * HEAD]


def pack(keys, values):
    rows, columns = keys.shape
    groups = columns // HEAD
    return pl.pallas_call(
        functools.partial(pack_kernel, groups),
        in_specs=[VMEM, VMEM],
        out_specs=VMEM,
        out_shape=jax.ShapeDtypeStruct((groups, 2, rows, HEAD), keys.dtype),
    )(keys, values)


def attend_kernel(plan, per_item, own, has_state, final, *refs):
    refs = list(refs)
    position_ref, q_ref, seg_ref = refs[:3]
    buffers = 1 + max(b for b, _, _ in plan)
    kv_refs = refs[3 : 3 + buffers]
    refs = refs[3 + buffers :]
    if has_state:
        acc_in, stat_in = refs[:2]
        refs = refs[2:]
    if final:
        out_ref = refs[0]
        refs = refs[1:]
    else:
        acc_out, stat_out = refs[:2]
        refs = refs[2:]
    k_s, vt_s, bias_s, one_s, s_s, p_s, t_s, acc_s, *rest = refs

    rows = q_ref.shape[0]
    heads = q_ref.shape[1] // HEAD
    count = len(plan)
    c = position_ref[0]
    parts = rows // HEAD
    q_seg = jnp.concatenate([seg_ref[pl.ds(parts * c + i, 1), :] for i in range(parts)], 1)
    first_seg = jnp.min(q_seg)
    start = jnp.sum((seg_ref[...] < first_seg).astype(jnp.int32))
    query_bias = jnp.where(q_seg == first_seg, 0.0, MASKED).astype(jnp.float32)
    for i, (b, slot, block_of) in enumerate(plan):
        src = kv_refs[b] if slot is None else kv_refs[b].at[slot]
        k_s[i * rows : (i + 1) * rows, :HEAD] = src[:, 0].reshape(rows, HEAD)
        vt_s[:, i * rows : (i + 1) * rows] = src[:, 1].reshape(rows, HEAD).T
        if own:
            key_seg = jnp.broadcast_to(q_seg.astype(jnp.float32), (rows, rows)).T
            k_pos = lax.broadcasted_iota(jnp.int32, (rows, rows), 0)
            q_pos = lax.broadcasted_iota(jnp.int32, (rows, rows), 1)
            allowed = (key_seg == q_seg.astype(jnp.float32)) & (k_pos <= q_pos)
            bias_s[...] = jnp.where(allowed, 0.0, MASKED).astype(jnp.float32)
        else:
            lane = lax.broadcasted_iota(jnp.int32, (rows, HEAD), 1)
            k_pos = block_of(c) * rows + lax.broadcasted_iota(jnp.int32, (rows, HEAD), 0)
            masked = (k_pos < start) & (lane == 0)
            k_s[i * rows : (i + 1) * rows, HEAD:] = jnp.where(masked, MASKED, 0.0).astype(
                jnp.bfloat16
            )
            one_s[...] = jnp.where(lane == 0, 1.0, 0.0).astype(jnp.bfloat16)

    splits = count // per_item
    items = [(h, g) for h in range(heads) for g in range(splits)]

    def score(t):
        h, g = items[t]
        q = q_ref[:, h * HEAD : (h + 1) * HEAD]
        if not own:
            q = jnp.concatenate([q, one_s[...]], 1)
        s_s[t % 4] = lax.dot_general(
            k_s[g * per_item * rows : (g + 1) * per_item * rows],
            q,
            NT,
            preferred_element_type=jnp.float32,
        )

    def soften(t):
        _, g = items[t]
        for i in range(per_item):
            x = s_s[t % 4, i * rows : (i + 1) * rows]
            if own:
                x = x + bias_s[...]
            top = jnp.max(x, 0, keepdims=True)
            expo = jnp.exp2((x - top) * EXP2_SCALE)
            t_s[t % 4, i : i + 1] = top if own else top + query_bias
            t_s[t % 4, 8 + i : 9 + i] = jnp.sum(expo, 0, keepdims=True)
            p_s[t % 4, i * rows : (i + 1) * rows] = expo.astype(jnp.bfloat16)

    def mix(t):
        h, g = items[t]
        tops = [t_s[t % 4, i : i + 1] for i in range(per_item)]
        totals = [t_s[t % 4, 8 + i : 9 + i] for i in range(per_item)]
        best = functools.reduce(jnp.maximum, tops)
        acc = total = None
        if g > 0:
            old = t_s[4 + h % 2, 0:1]
            best = jnp.maximum(best, old)
            f = jnp.exp2((old - best) * EXP2_SCALE)
            acc, total = acc_s[h % 2] * f, t_s[4 + h % 2, 8:9] * f
        elif has_state:
            old = stat_in[h, 0:1]
            best = jnp.maximum(best, old)
            f = jnp.exp2((old - best) * EXP2_SCALE)
            acc, total = acc_in[h] * f, stat_in[h, 1:2] * f
        for i in range(per_item):
            at = (g * per_item + i) * rows
            part = jnp.dot(
                vt_s[:, at : at + rows],
                p_s[t % 4, i * rows : (i + 1) * rows],
                preferred_element_type=jnp.float32,
            )
            f = jnp.exp2((tops[i] - best) * EXP2_SCALE)
            acc = part * f if acc is None else acc + part * f
            total = totals[i] * f if total is None else total + totals[i] * f
        if g < splits - 1:
            acc_s[h % 2] = acc
            t_s[4 + h % 2, 0:1] = best
            t_s[4 + h % 2, 8:9] = total
        elif final:
            out_s, sems = rest
            out_s[h] = (acc / total).astype(jnp.bfloat16).T
            copies.append(
                pltpu.make_async_copy(
                    out_s.at[h], out_ref.at[:, h * HEAD : (h + 1) * HEAD], sems.at[h]
                )
            )
            copies[-1].start()
        else:
            acc_out[h] = acc
            stat_out[h, 0:1] = best
            stat_out[h, 1:2] = total

    copies = []
    for t in range(len(items) + 2):
        if t < len(items):
            score(t)
        if 1 <= t <= len(items):
            soften(t - 1)
        if t >= 2:
            mix(t - 2)
    for copy in copies:
        copy.wait()


def attend(position, queries, segments, buffers, plan, per_item, own=False, state=(), final=False):
    rows, columns = queries.shape
    heads = columns // HEAD
    count = len(plan)
    if final:
        out_shape = jax.ShapeDtypeStruct(queries.shape, queries.dtype)
        out_specs = pl.BlockSpec(memory_space=pl.ANY)
    else:
        out_shape = [
            jax.ShapeDtypeStruct((heads, HEAD, rows), jnp.float32),
            jax.ShapeDtypeStruct((heads, 8, rows), jnp.float32),
        ]
        out_specs = [VMEM, VMEM]
    return pl.pallas_call(
        functools.partial(attend_kernel, plan, per_item, own, bool(state), final),
        in_specs=[SMEM] + [VMEM] * (2 + len(buffers) + len(state)),
        out_specs=out_specs,
        out_shape=out_shape,
        scratch_shapes=[
            pltpu.VMEM((count * rows, HEAD if own else 2 * HEAD), jnp.bfloat16),
            pltpu.VMEM((HEAD, count * rows), jnp.bfloat16),
            pltpu.VMEM((rows, rows if own else HEAD), jnp.float32),
            pltpu.VMEM((rows, HEAD), jnp.bfloat16),
            pltpu.VMEM((4, per_item * rows, rows), jnp.float32),
            pltpu.VMEM((4, per_item * rows, rows), jnp.bfloat16),
            pltpu.VMEM((6, 16, rows), jnp.float32),
            pltpu.VMEM((2, HEAD, rows), jnp.float32),
        ]
        + (
            [pltpu.VMEM((heads, rows, HEAD), queries.dtype), pltpu.SemaphoreType.DMA((heads,))]
            if final
            else []
        ),
        compiler_params=pltpu.CompilerParams(vmem_limit_bytes=24 << 20),
        cost_estimate=pl.CostEstimate(
            flops=4 * heads * rows * rows * HEAD * count,
            bytes_accessed=4 * rows * columns,
            transcendentals=heads * rows * rows * count,
        ),
    )(position, queries, segments, *buffers, *state)


def own_block(c):
    return c


def back_block(distance, c):
    return c - distance


def near_row(shift, c):
    y = lax.rem(c, WIDE)
    source = lax.rem(y - shift + WIDE, WIDE)
    return c - y + source - WIDE


def edge_row(shift, c):
    y = lax.rem(c, WIDE)
    source = lax.rem(y - shift + WIDE, WIDE)
    return c - y + source - jnp.where(source < y, 0, 2 * WIDE)


def on_device(queries, keys, values, segment_ids):
    rows = queries.shape[0]
    blocks = lax.axis_size("ctx")
    position = lax.axis_index("ctx").astype(jnp.int32).reshape(1)
    segments = segment_ids.reshape(-1, HEAD)
    own = lax.all_to_all(pack(keys, values), "kvg", split_axis=0, concat_axis=0, tiled=True)

    def back(block, distance):
        return lax.ppermute(block, "ctx", [(i, (i + distance) % blocks) for i in range(blocks)])

    def around(block, shift):
        return lax.ppermute(
            block, "ctx", [(i, i - i % WIDE + (i + shift) % WIDE) for i in range(blocks)]
        )

    y = lax.rem(position[0], WIDE)
    near = back(own, WIDE)
    state = attend(position, queries, segments, [own], [(0, None, own_block)], 1, own=True)
    near, state = lax.optimization_barrier((near, state))
    shifts = (1, 3, 2)
    near_arrived = [around(near, shift) for shift in shifts]
    far = back(near, WIDE)
    edge_arrived = [
        around(jnp.where(y < lax.rem(y + shift, WIDE), own, far), shift) for shift in shifts
    ]
    plan = [
        (0, None, functools.partial(back_block, WIDE)),
        (1, None, functools.partial(back_block, 2 * WIDE)),
    ]
    plan += [(2 + i, None, functools.partial(near_row, shift)) for i, shift in enumerate(shifts)]
    state = attend(position, queries, segments, [near, far, *near_arrived], plan, 5, state=state)
    plan = [(i, None, functools.partial(edge_row, shift)) for i, shift in enumerate(shifts)]
    return attend(position, queries, segments, edge_arrived, plan, 3, state=state, final=True)


def solution(mesh):
    return jax.shard_map(
        on_device,
        mesh=mesh,
        in_specs=(P("ctx", "kvg"), P(("ctx", "kvg"), None), P(("ctx", "kvg"), None), P()),
        out_specs=P("ctx", "kvg"),
        check_vma=False,
    )
```
